32 devices in a mesh: rep: 2 (over y), pool: 4 (over x, core), tp: 4 (over z).
Axes of the slice: x: 2, y: 2, z: 4, core: 2. Of those that a mesh axis runs over, the one named last changes fastest.
Arguments:
- prompt_states: bfloat16 [12288, 16384], P(('rep', 'pool'), 'tp'), parts along dimension 0, may hold values from -6 to 6
- kv_weight: bfloat16 [16384, 2048], P('tp'), may hold values from -0.046875 to 0.046875
- prompt_lens: int32 [8, 12], P(('rep', 'pool')), parts along dimension 0, may hold values from 1 to 128, 1152 in all within a row
- placement: int32 [96, 1], P(('rep', 'pool')), parts along dimension 0, may hold values from 0 to 3; in each aligned block of 12 rows (0 to 11, 12 to 23, ...) at most 6 rows name the same one
- old_cache: bfloat16 [128, 192, 2048], P(('rep', 'pool'), None, 'tp'), parts along dimension 0, may hold values from -4 to 4
- old_lens: int32 [8, 16], P(('rep', 'pool')), parts along dimension 0, may hold values from 1 to 192, 1536 in all within a row
- query_old: bfloat16 [4, 128, 16384], P(None, ('rep', 'pool'), 'tp'), parts along dimension 1, may hold values from -120 to 120
- step_old: bfloat16 [4, 128, 2048], P(None, ('rep', 'pool'), 'tp'), parts along dimension 1, may hold values from -4 to 4
- query_new: bfloat16 [4, 192, 16384], P(None, ('rep', 'pool'), 'tp'), parts along dimension 1, may hold values from -120 to 120
- step_new: bfloat16 [4, 192, 2048], P(None, ('rep', 'pool'), 'tp'), parts along dimension 1, may hold values from -4 to 4
Outputs:
- attn_old: bfloat16 [4, 128, 16384], P(None, ('rep', 'pool'), 'tp'), parts along dimension 1
- attn_new: bfloat16 [4, 192, 16384], P(None, ('rep', 'pool'), 'tp'), parts along dimension 1
The draws below stay inside these ranges and needn't reach their ends.
There are 2 independent parts, one for each index of `rep`. The reference program is written for one: setup_inputs(seed, part) draws one part's arguments, and reference() takes and returns one part's arrays. A program takes and returns all parts, laid end to end along the dimension named above; an argument that names none is the same for every part. Nothing has to cross between parts.
Inputs may be any that keep to these rules, and one draw needn't show every extreme that they name: `placement`: at most 6 of the 12 prompts of one pool index name the same decode index, and this is reached.
All inputs are finite; a program needn't handle non-finite values.
Results may differ from the reference program's by a relative error of at most 0.019.
Values may be sent and summed in bfloat16 or wider, within the bound.
A program may use at most 128 MiB of HBM per device.

```python
import math
import jax
import jax.numpy as jnp
import numpy as np
from jax import lax

D = 16384
QH = 128
KVH = 8
HD = 128
QPK = 16
PD = 12
PLEN = 128
OLD = 16
CTX = 192
STEPS = 4
CAP = 6
PROMPTS = 48
TOKENS = 6144
OLD_ALL = 64
SLOTS_ALL = 96
N_POOL = 4
N_TP = 4


def shared_keys(key, count, marker):
    key = jax.random.fold_in(key, marker)
    return jnp.clip(jax.random.normal(key, (STEPS, count, KVH, HD), jnp.float32), -4.0, 4.0)


def draw_query_old(key, part):
    key = jax.random.fold_in(key, 1)
    first = jax.random.fold_in(key, 0)
    drawn = jnp.clip(jax.random.normal(first, (STEPS, OLD_ALL, KVH, QPK, HD), jnp.float32), -4.0, 4.0)
    return drawn.reshape(STEPS, OLD_ALL, QH * HD).astype(jnp.bfloat16)


def draw_step_old(key, part):
    keys = shared_keys(key, OLD_ALL, 101)
    key = jax.random.fold_in(key, 2)
    values = jnp.clip(jax.random.normal(key, (STEPS, OLD_ALL, KVH, HD), jnp.float32), -4.0, 4.0)
    return jnp.stack([keys, values], axis=3).reshape(STEPS, OLD_ALL, 2 * KVH * HD).astype(jnp.bfloat16)


def draw_query_new(key, part):
    key = jax.random.fold_in(key, 3)
    first = jax.random.fold_in(key, 0)
    drawn = jnp.clip(jax.random.normal(first, (STEPS, SLOTS_ALL, KVH, QPK, HD), jnp.float32), -4.0, 4.0)
    return drawn.reshape(STEPS, SLOTS_ALL, QH * HD).astype(jnp.bfloat16)


def draw_step_new(key, part):
    keys = shared_keys(key, SLOTS_ALL, 202)
    key = jax.random.fold_in(key, 4)
    values = jnp.clip(jax.random.normal(key, (STEPS, SLOTS_ALL, KVH, HD), jnp.float32), -4.0, 4.0)
    return jnp.stack([keys, values], axis=3).reshape(STEPS, SLOTS_ALL, 2 * KVH * HD).astype(jnp.bfloat16)


def block_levels(key, extent, shards, smallest, largest):
    gain, own = 1.0, jax.random.fold_in(key, 6)
    for dim, parts in shards:
        heights = jnp.exp(jax.random.uniform(jax.random.fold_in(own, dim), (parts,), jnp.float32, smallest / len(shards), largest / len(shards)))
        gain = gain * jnp.repeat(heights, extent[dim] // parts).reshape([-1 if axis == dim else 1 for axis in range(len(extent))])
    return gain


def split_up(number_of, total, most, slope):
    loads = [(1 << 20) // math.isqrt(rank ** slope) + 1 for rank in range(2, number_of + 1)]
    spare, counts = total - most - (number_of - 1), [1] * (number_of - 1)
    while spare > 0:
        free = [i for i in range(number_of - 1) if counts[i] < most]
        mass, remaining = sum([loads[i] for i in free]), spare
        for i in free:
            addition = min(most - counts[i], max(1, remaining * loads[i] // mass), spare)
            counts[i] = counts[i] + addition
            spare = spare - addition
    return np.array([most] + counts)


def ragged_sizes(stream_key, count, total, most, lean):
    if count == 2:
        one = jax.random.randint(stream_key, (), max(1, total - most), min(most, total - 1) + 1)
        return jnp.stack([one, total - one])
    tallies = jnp.asarray(split_up(count, total, most, lean), jnp.int32)
    pairs = (count - 1) // 2
    donor, receiver = tallies[1:1 + 2 * pairs:2], tallies[2:2 + 2 * pairs:2]
    room = jnp.minimum(donor - 1, most - receiver)
    moved = jax.random.randint(jax.random.fold_in(stream_key, 1), (pairs,), 0, 1 << 20) % (room + 1)
    tallies = tallies.at[1:1 + 2 * pairs:2].set(donor - moved).at[2:2 + 2 * pairs:2].set(receiver + moved)
    return tallies[jax.random.permutation(jax.random.fold_in(stream_key, 2), count)]


def shared_out(own_key, own, number, rows, count, top, reach, slope):
    sequence = jax.random.permutation(own_key, count)
    packed, common = portions_of(count, rows * top, reach, slope, True), portions_of(count, rows * top, reach, slope, False)
    places = jnp.arange(count)

    def named(lengths, offset_by):
        used = int((lengths > 0).sum())
        fixed = max(1, used // 4)
        shifted = fixed + (places - fixed + offset_by * (used - fixed)) % max(1, count - fixed)
        return jnp.zeros((count,), jnp.int32).at[sequence[jnp.where(places < fixed, places, shifted)]].set(jnp.asarray(lengths, jnp.int32))

    lengths = jnp.where(number % 4 == 0, named(packed, number // 4), named(common, number - number // 4 - 1))
    mixed = jax.random.permutation(jax.random.fold_in(own, 3), count)
    giver, receiver = mixed[0:count // 2 * 2:2], mixed[1:count // 2 * 2:2]
    margin = jnp.minimum(lengths[giver] - 1, reach - lengths[receiver]) // 2
    margin = jnp.where((giver == sequence[0]) | (receiver == sequence[0]) | (lengths[receiver] == 0), 0, jnp.maximum(margin, 0))
    shifted = jax.random.randint(jax.random.fold_in(own, 4), (count // 2,), 0, 1 << 20) % (margin + 1)
    lengths = lengths.at[giver].add(-shifted).at[receiver].add(shifted)
    labels = jnp.searchsorted(jnp.cumsum(lengths), jnp.arange(rows * top), side="right").astype(jnp.int32)
    grid = labels.reshape(top, rows).T
    grid = grid[jax.random.permutation(jax.random.fold_in(own, 1), rows)]
    offset_by = jax.random.randint(jax.random.fold_in(own, 2), (rows, 1), 0, top)
    return jnp.take_along_axis(grid, (jnp.arange(top)[None, :] + offset_by) % top, axis=1)


def portions_of(amount, total, most, lean, full):
    weights = [(1 << 20) // math.isqrt(rank ** lean) + 1 for rank in range(1, amount + 1)]
    largest = most if full else min(most, max(-(-total // amount), total * weights[0] // sum(weights)))
    least = 1 if total - largest >= amount - 1 else 0
    given, spare = [largest] + [least] * (amount - 1), total - largest - least * (amount - 1)
    while spare > 0:
        candidates = [i for i in range(1, amount) if given[i] < largest] or [i for i in range(1, amount) if given[i] < most]
        pool, budget = sum([weights[i] for i in candidates]), spare
        for i in candidates:
            more = min(most - given[i], max(1, budget * weights[i] // pool), spare)
            given[i] = given[i] + more
            spare = spare - more
    return np.array(given)


def normal_values(own_key, shape, scale, reach, shards=(), kind=jnp.bfloat16):
    loudness = block_levels(own_key, shape, shards, -0.22, 0.18) if shards else 1.0
    values = jax.random.normal(own_key, shape, jnp.float32) * scale * loudness
    return jnp.minimum(jnp.maximum(values, -reach), reach).astype(kind)


def setup_inputs(seed: int = 0, part: int = 0) -> dict:
    splits = jax.random.split(jax.random.key(seed), 11)
    part_keys = jax.random.split(jax.random.fold_in(splits[10], part), 11)
    prompt_states = normal_values(part_keys[0], (TOKENS, D), 1.0, 6.0, ((0, 4), (1, 4)))
    kv_weight = normal_values(splits[1], (D, 2 * KVH * HD), D ** -0.5, 0.046875, ((0, 4),))
    prompt_lens = jax.vmap(lambda own: ragged_sizes(own, PD, PD * PLEN * 3 // 4, PLEN, 2))(jax.random.split(part_keys[2], N_POOL)).reshape((N_POOL, PD)).astype(jnp.int32)
    placement_keys = jax.random.split(jax.random.fold_in(part_keys[3], 1), PROMPTS // PD)
    placement_turns = jax.random.permutation(jax.random.fold_in(part_keys[3], 3), PROMPTS // PD)
    placement = jax.vmap(lambda own, number: shared_out(jax.random.fold_in(part_keys[3], 2), own, number, PD, N_POOL, 1, CAP, 2))(placement_keys, placement_turns).reshape((PROMPTS, 1))
    old_cache = normal_values(part_keys[4], (OLD_ALL, CTX, 2 * KVH * HD), 1.0, 4.0, ((0, 4), (2, 4)))
    old_lens = jax.vmap(lambda own: ragged_sizes(own, OLD, OLD * CTX // 2, CTX, 2))(jax.random.split(part_keys[5], N_POOL)).reshape((N_POOL, OLD)).astype(jnp.int32)
    query_old = draw_query_old(jax.random.fold_in(jax.random.fold_in(splits[10], part), 71), part)
    step_old = draw_step_old(jax.random.fold_in(jax.random.fold_in(splits[10], part), 71), part)
    query_new = draw_query_new(jax.random.fold_in(jax.random.fold_in(splits[10], part), 71), part)
    step_new = draw_step_new(jax.random.fold_in(jax.random.fold_in(splits[10], part), 71), part)
    return {"prompt_states": prompt_states, "kv_weight": kv_weight, "prompt_lens": prompt_lens, "placement": placement, "old_cache": old_cache, "old_lens": old_lens, "query_old": query_old, "step_old": step_old, "query_new": query_new, "step_new": step_new}


def rotate(vec, pos):
    size = vec.shape[-1]
    half = size // 2
    idx = jnp.arange(half, dtype=jnp.float32)
    freq = jnp.exp(-(2.0 * idx / size) * math.log(500000.0))
    angle = pos[..., None].astype(jnp.float32) * freq
    cosine = jnp.cos(angle)
    sine = jnp.sin(angle)
    first = vec[..., :half]
    second = vec[..., half:]
    return jnp.concatenate([first * cosine - second * sine, second * cosine + first * sine], axis=-1)

def decode(query, cache_k, cache_v, lens, step_kv):
    steps, count = (query.shape[0], query.shape[1])
    heads, width = (cache_k.shape[2], cache_k.shape[3])
    group = query.shape[2] // (heads * width)
    pos = lens[None, :] + jnp.arange(steps, dtype=jnp.int32)[:, None]
    q_rot = rotate(query.reshape(steps, count, heads, group, width).astype(jnp.float32), pos[:, :, None, None]).astype(jnp.bfloat16)
    pairs = step_kv.reshape(steps, count, heads, 2, width)
    s_key = rotate(pairs[:, :, :, 0].astype(jnp.float32), pos[:, :, None]).astype(jnp.bfloat16)
    s_val = pairs[:, :, :, 1]
    scale = 1.0 / math.sqrt(width)
    sc_cache = jnp.einsum('sbhqd,blhd->sbhql', q_rot.astype(jnp.float32), cache_k.astype(jnp.float32)) * scale
    sc_step = jnp.einsum('sbhqd,tbhd->sbhqt', q_rot.astype(jnp.float32), s_key.astype(jnp.float32)) * scale
    rows = cache_k.shape[1]
    mask_cache = (jnp.arange(rows, dtype=jnp.int32)[None, :] < lens[:, None])[None, :, None, None, :]
    mask_step = (jnp.arange(steps, dtype=jnp.int32)[None, :] <= jnp.arange(steps, dtype=jnp.int32)[:, None])[:, None, None, None, :]
    low = jnp.float32(-1e+30)
    sc_cache = jnp.where(mask_cache, sc_cache, low)
    sc_step = jnp.where(mask_step, sc_step, low)
    top = jnp.maximum(lax.optimization_barrier(jnp.max(sc_cache, axis=-1)), lax.optimization_barrier(jnp.max(sc_step, axis=-1)))[..., None]
    ex_cache = jnp.where(mask_cache, jnp.exp(sc_cache - top), 0.0)
    ex_step = jnp.where(mask_step, jnp.exp(sc_step - top), 0.0)
    total = lax.optimization_barrier(jnp.sum(ex_cache, axis=-1, keepdims=True)) + lax.optimization_barrier(jnp.sum(ex_step, axis=-1, keepdims=True))
    w_cache = (ex_cache / total).astype(jnp.bfloat16)
    w_step = (ex_step / total).astype(jnp.bfloat16)
    out = jnp.einsum('sbhql,blhd->sbhqd', w_cache.astype(jnp.float32), cache_v.astype(jnp.float32))
    out = out + jnp.einsum('sbhqt,tbhd->sbhqd', w_step.astype(jnp.float32), s_val.astype(jnp.float32))
    return out.reshape(steps, count, heads * group * width).astype(jnp.bfloat16)

def reference(prompt_states, kv_weight, prompt_lens, placement, old_cache, old_lens, query_old, step_old, query_new, step_new):
    block = D // N_TP
    kv_proj = jnp.zeros((TOKENS, 2 * KVH * HD), jnp.float32)
    for piece in range(N_TP):
        part = jnp.dot(prompt_states[:, piece * block:(piece + 1) * block], kv_weight[piece * block:(piece + 1) * block], preferred_element_type=jnp.float32)
        kv_proj = kv_proj + lax.optimization_barrier(part.astype(jnp.bfloat16)).astype(jnp.float32)
    kv_proj = kv_proj.reshape(TOKENS, KVH, 2, HD)
    position = jnp.arange(TOKENS, dtype=jnp.int32) % PLEN
    keys = rotate(kv_proj[:, :, 0], position[:, None]).astype(jnp.bfloat16)
    values = kv_proj[:, :, 1].astype(jnp.bfloat16)
    prompt_cache = jnp.stack([keys, values], axis=2).reshape(PROMPTS, PLEN, KVH, 2, HD)
    dest = placement[:, 0]
    onehot = (dest[:, None] == jnp.arange(N_POOL, dtype=jnp.int32)[None, :]).astype(jnp.int32).reshape(N_POOL, PD, N_POOL)
    before = jnp.cumsum(onehot, axis=1) - onehot
    rank = lax.optimization_barrier(jnp.sum(before * onehot, axis=2)).reshape(PROMPTS)
    source = jnp.arange(PROMPTS, dtype=jnp.int32) // PD
    slot = dest * (N_POOL * CAP) + source * CAP + rank
    new_cache = jnp.zeros((SLOTS_ALL, PLEN, KVH, 2, HD), jnp.bfloat16).at[slot].set(prompt_cache)
    new_lens = jnp.zeros((SLOTS_ALL,), jnp.int32).at[slot].set(prompt_lens.reshape(PROMPTS))
    resident = old_cache.reshape(OLD_ALL, CTX, KVH, 2, HD)
    attn_old = decode(query_old, resident[:, :, :, 0], resident[:, :, :, 1], old_lens.reshape(OLD_ALL), step_old)
    attn_new = decode(query_new, new_cache[:, :, :, 0], new_cache[:, :, :, 1], new_lens, step_new)
    return (attn_old, attn_new)
```

```python
import functools
import math

import jax
import jax.numpy as jnp
import numpy as np
from jax import lax
from jax.experimental import pallas as pl
from jax.experimental.pallas import tpu as pltpu
from jax.sharding import PartitionSpec as P

HD = 128
PIECES = 3
MESH = pl.DeviceIdType.MESH
F32 = jnp.float32
BF16 = jnp.bfloat16


def turn(v, cosine, sine):
    return v * cosine + pltpu.roll(v, HD // 2, v.ndim - 1) * sine


def tables(pos):
    half = HD // 2
    freq = jnp.exp(-(2.0 * jnp.arange(half, dtype=F32) / HD) * math.log(500000.0))
    angle = pos[..., None].astype(F32) * freq
    c, s = jnp.cos(angle), jnp.sin(angle)
    return jnp.concatenate([c, c, -s, s], axis=-1)


def kernel(
    dims,
    x, w, target, ptab, q_old, s_old, cache, tab_old, q_new, s_new, tab_new,
    len_old, off_new, len_new,
    o_old, o_new,
    wbuf, y, pick, part, rbuf, qs, ks, vs, os_, store, *rest,
):
    n, pool, heads, group, plen, cap, rows, packed = dims
    pbuf = rest[:heads]
    wsem, zsend, zrecv, agsend, agrecv, fwsend = rest[heads:]
    z, me = lax.axis_index("tp"), lax.axis_index("pool")
    chips = pool // 2
    chip, core = me // 2, lax.rem(me, 2)
    mate = chip * 2 + 1 - core
    size = packed // PIECES
    slack = rows - packed
    steps = q_old.shape[0]

    def peer(k):
        return lax.rem(chip + k, chips) * 2 + core

    def source(k):
        return lax.rem(chip + chips - k, chips) * 2 + core

    def order(k):
        middle = n - 1 - k // 2 if k % 2 == 0 else (k - 1) // 2
        return jnp.where(z == 0, n - 1 - k, jnp.where(z == n - 1, k, middle))

    blocks = [(h, k) for h in range(heads) for k in range(n)]

    def weights(i):
        h, k = blocks[i]
        first = pl.multiple_of((order(k) * heads + h) * 2 * HD, 2 * HD)
        return pltpu.make_async_copy(
            w.at[:, pl.ds(first, 2 * HD)], wbuf.at[i % 2], wsem.at[i % 2]
        )

    weights(0).start()

    barrier = pltpu.get_barrier_semaphore()

    @pl.when(z > 0)
    def _():
        pl.semaphore_signal(barrier, inc=1, device_id={"tp": z - 1}, device_id_type=MESH)

    @pl.when(z < n - 1)
    def _():
        pl.semaphore_signal(barrier, inc=1, device_id={"tp": z + 1}, device_id_type=MESH)

    pl.semaphore_signal(barrier, inc=1, device_id={"pool": mate}, device_id_type=MESH)
    for k in range(1, chips):
        pl.semaphore_signal(barrier, inc=1, device_id={"pool": peer(k)}, device_id_type=MESH)
    for p in range(PIECES):
        wanted = target[:, p * size : (p + 1) * size + slack]
        line = lax.broadcasted_iota(jnp.int32, (size, size + slack), 0) + p * size
        pick[p] = jnp.where(line == wanted, 1.0, 0.0).astype(BF16)
    ks[...] = jnp.zeros_like(ks)
    vs[...] = jnp.zeros_like(vs)
    edges = (z > 0).astype(jnp.int32) + (z < n - 1).astype(jnp.int32)
    pl.semaphore_wait(barrier, edges + chips)

    def span(p):
        return pl.ds(p * size, size)

    def up(d, h, p):
        return pltpu.make_async_remote_copy(
            part.at[d, h, span(p)], rbuf.at[0, d, h, span(p)],
            zsend.at[d, h, p], zrecv.at[0, d, h, p],
            device_id={"tp": z + 1}, device_id_type=MESH,
        )

    def down(d, h, p):
        return pltpu.make_async_remote_copy(
            part.at[d, h, span(p)], rbuf.at[1, d, h, span(p)],
            zsend.at[d, h, p], zrecv.at[1, d, h, p],
            device_id={"tp": z - 1}, device_id_type=MESH,
        )

    def share(h, p, k):
        return pltpu.make_async_remote_copy(
            pbuf[h].at[me, span(p)], pbuf[h].at[me, span(p)],
            agsend.at[k, h, p], agrecv.at[me, h, p],
            device_id={"pool": mate if k == 0 else peer(k)}, device_id_type=MESH,
        )

    def forward(h, p, k):
        src = source(k)
        return pltpu.make_async_remote_copy(
            pbuf[h].at[src, span(p)], pbuf[h].at[src, span(p)],
            fwsend.at[k, h, p], agrecv.at[src, h, p],
            device_id={"pool": mate}, device_id_type=MESH,
        )

    def arrived(h, p, src):
        return pltpu.make_async_remote_copy(
            pbuf[h].at[src, span(p)], pbuf[h].at[src, span(p)],
            fwsend.at[0, h, p], agrecv.at[src, h, p],
            device_id={"pool": mate}, device_id_type=MESH,
        )

    def multiply(i):
        h, k = blocks[i]
        d = order(k)
        if i + 1 < len(blocks):
            weights(i + 1).start()
        weights(i).wait()
        tile = 4 * plen

        def body(r, carry):
            at = pl.ds(pl.multiple_of(r * tile, tile), tile)
            got = jnp.dot(x[at, :], wbuf[i % 2], preferred_element_type=F32)
            y[at, HD:] = got[:, HD:].astype(BF16)
            key = got[:, :HD].reshape(4, plen, HD)
            key = turn(key, ptab[:, :HD][None], ptab[:, HD:][None])
            y[at, :HD] = key.reshape(tile, HD).astype(BF16)
            return carry

        lax.fori_loop(0, rows // tile, body, 0)
        for p in range(PIECES):
            part[d, h, span(p)] = jnp.dot(
                pick[p], y[p * size : (p + 1) * size + slack], preferred_element_type=F32
            ).astype(BF16)

            @pl.when((z == 0) & (d > 0))
            def _():
                up(d, h, p).start()

            @pl.when((z == n - 1) & (d < n - 1))
            def _():
                down(d, h, p).start()

    def relay(h, s):
        for p in range(PIECES):
            high, low = n - 1 - s, s

            @pl.when((z > 0) & (z < high))
            def _():
                up(high, h, p).wait_recv()
                part[high, h, span(p)] = (
                    part[high, h, span(p)].astype(F32) + rbuf[0, high, h, span(p)].astype(F32)
                ).astype(BF16)
                up(high, h, p).start()

            @pl.when((z < n - 1) & (z > low))
            def _():
                down(low, h, p).wait_recv()
                part[low, h, span(p)] = (
                    part[low, h, span(p)].astype(F32) + rbuf[1, low, h, span(p)].astype(F32)
                ).astype(BF16)
                down(low, h, p).start()

            last = jnp.maximum(
                jnp.where(z > 0, n - 1 - z, 0), jnp.where(z < n - 1, z, 0)
            )

            @pl.when(last == s)
            def _():
                mine = pbuf[h].at[me, span(p)]

                @pl.when(z == 0)
                def _():
                    down(z, h, p).wait_recv()
                    mine[...] = (
                        part[z, h, span(p)].astype(F32) + rbuf[1, z, h, span(p)].astype(F32)
                    ).astype(BF16)

                @pl.when(z == n - 1)
                def _():
                    up(z, h, p).wait_recv()
                    mine[...] = (
                        part[z, h, span(p)].astype(F32) + rbuf[0, z, h, span(p)].astype(F32)
                    ).astype(BF16)

                @pl.when((z > 0) & (z < n - 1))
                def _():
                    up(z, h, p).wait_recv()
                    down(z, h, p).wait_recv()
                    mine[...] = (
                        part[z, h, span(p)].astype(F32)
                        + rbuf[0, z, h, span(p)].astype(F32)
                        + rbuf[1, z, h, span(p)].astype(F32)
                    ).astype(BF16)

                for k in range(chips):
                    share(h, p, k).start()

    def spread(h):
        for p in range(PIECES):
            for k in range(1, chips):
                arrived(h, p, source(k)).wait_recv()
                forward(h, p, k).start()

    def collect(h):
        for p in range(PIECES):
            for k in range(chips):
                arrived(h, p, lax.rem(chip + k, chips) * 2 + 1 - core).wait_recv()

    def attend(h, q, st, tab, out, block, width, per, count):
        for t in range(steps):
            c, s = tab[t, :, :HD], tab[t, :, HD:]
            for g in range(group):
                col = (h * group + g) * HD
                at = (t * group + g) * count
                qs[at : at + count, :] = turn(q[t, :, col : col + HD].astype(F32), c, s)
            col = h * 2 * HD
            ks[t * count : (t + 1) * count, :] = turn(st[t, :, col : col + HD].astype(F32), c, s)
            vs[t * count : (t + 1) * count, :] = st[t, :, col + HD : col + 2 * HD].astype(F32)
        if count * steps < ks.shape[0]:
            ks[count * steps :, :] = jnp.zeros((ks.shape[0] - count * steps, HD), F32)
            vs[count * steps :, :] = jnp.zeros((ks.shape[0] - count * steps, HD), F32)
        m = steps * group
        col = lax.broadcasted_iota(jnp.int32, (m, width + 16), 1)
        now = lax.broadcasted_iota(jnp.int32, (m, width + 16), 0) // group
        recent = (col >= width) & (col - width <= now)

        def body(i, carry):
            for j in range(per):
                b = i * per + j
                kv, low, high = block(b, h)
                query = qs[pl.ds(b, m, stride=count), :].astype(BF16)
                own_k = ks[pl.ds(b, 16, stride=count), :].astype(BF16)
                own_v = vs[pl.ds(b, 16, stride=count), :].astype(BF16)
                keys = jnp.concatenate([kv[:, :HD], own_k], axis=0)
                values = jnp.concatenate([kv[:, HD:], own_v], axis=0)
                score = lax.dot_general(
                    query, keys, (((1,), (1,)), ((), ())), preferred_element_type=F32
                ) * (1.0 / math.sqrt(HD))
                keep = ((col >= low) & (col < high)) | recent
                score = jnp.where(keep, score, -1e30)
                top = jnp.max(score, axis=-1, keepdims=True)
                e = jnp.where(keep, jnp.exp(score - top), 0.0)
                total = jnp.sum(e, axis=-1, keepdims=True)
                got = jnp.dot((e / total).astype(BF16), values, preferred_element_type=F32)
                os_[pl.ds(b, m, stride=count), :] = got
            return carry

        lax.fori_loop(0, count // per, body, 0)
        for t in range(steps):
            for g in range(group):
                c0 = (h * group + g) * HD
                at = (t * group + g) * count
                out[t, :, c0 : c0 + HD] = os_[at : at + count, :].astype(BF16)

    def resident(b, h):
        return cache[b, :, h * 2 * HD : (h + 1) * 2 * HD], 0, len_old[b]

    def placed(b, h):
        return store[b], 0, len_new[b]

    def place(h):
        ahead = lax.broadcasted_iota(jnp.int32, (plen, packed), 1) - lax.broadcasted_iota(
            jnp.int32, (plen, packed), 0
        )

        def body(s, carry):
            got = pbuf[h][s]
            chosen = jnp.concatenate(
                [
                    jnp.where(ahead == off_new[s * cap + j], 1.0, 0.0).astype(BF16)
                    for j in range(cap)
                ],
                axis=0,
            )
            rows_of = jnp.dot(chosen, got, preferred_element_type=F32).astype(BF16)
            for j in range(cap):
                store[s * cap + j] = rows_of[j * plen : (j + 1) * plen]
            return carry

        lax.fori_loop(0, pool, body, 0)

    def old(h):
        attend(h, q_old, s_old, tab_old, o_old, resident, cache.shape[1], 4, q_old.shape[1])

    def new(h):
        collect(h)
        place(h)
        attend(h, q_new, s_new, tab_new, o_new, placed, plen, 4, q_new.shape[1])

    for i in range(n):
        multiply(i)
    later = []
    for h in range(heads):
        ahead = list(range((h + 1) * n, (h + 2) * n)) if h + 1 < heads else []
        for s in range(n - 1):
            relay(h, s)
            if ahead:
                multiply(ahead.pop(0))
            elif later:
                later.pop(0)()
        for i in ahead:
            multiply(i)
        spread(h)
        if h == 0:
            for g in range(heads):
                later.append(functools.partial(old, g))
            if heads > 1:
                later.pop(0)()
        later.append(functools.partial(new, h))
    for f in later:
        f()

    for h in range(heads):
        for p in range(PIECES):
            for d in range(n):

                @pl.when(z < d)
                def _():
                    up(d, h, p).wait_send()

                @pl.when(z > d)
                def _():
                    down(d, h, p).wait_send()

            for k in range(chips):
                share(h, p, k).wait_send()
            for k in range(1, chips):
                forward(h, p, k).wait_send()


def local(
    prompt_states,
    kv_weight,
    prompt_lens,
    placement,
    old_cache,
    old_lens,
    query_old,
    step_old,
    query_new,
    step_new,
):
    rows = prompt_states.shape[0]
    n, pool = lax.axis_size("tp"), lax.axis_size("pool")
    prompts = prompt_lens.shape[1]
    plen = rows // prompts
    packed = rows * 3 // 4
    heads = kv_weight.shape[1] // n // (2 * HD)
    group = query_old.shape[2] // (heads * HD)
    steps, olds = query_old.shape[:2]
    slots = query_new.shape[1]
    cap = slots // pool

    lens = prompt_lens[0]
    begin = jnp.cumsum(lens) - lens
    k = jnp.arange(plen, dtype=jnp.int32)[None]
    target = jnp.where(k < lens[:, None], begin[:, None] + k, -1).reshape(1, rows)

    meta = lax.all_gather(jnp.stack([lens, placement[:, 0]]), "pool")
    all_lens, dest = meta[:, 0], meta[:, 1]
    all_begin = jnp.cumsum(all_lens, axis=1) - all_lens
    here = (dest == lax.axis_index("pool")).astype(jnp.int32)
    rank = jnp.cumsum(here, axis=1) - here
    hit = (here[:, None, :] > 0) & (
        rank[:, None, :] == jnp.arange(cap, dtype=jnp.int32)[None, :, None]
    )
    len_new = jnp.sum(jnp.where(hit, all_lens[:, None], 0), axis=2).reshape(slots)
    off_new = jnp.sum(jnp.where(hit, all_begin[:, None], 0), axis=2).reshape(slots)
    t = jnp.arange(steps, dtype=jnp.int32)[:, None]
    tab_old = tables(old_lens + t)
    tab_new = tables(len_new[None] + t)
    half = HD // 2
    angle = np.arange(plen, dtype=np.float32)[:, None] * np.exp(
        -(2.0 * np.arange(half, dtype=np.float32) / HD) * np.float32(math.log(500000.0))
    ).astype(np.float32)
    c, s = np.cos(angle), np.sin(angle)
    ptab = jnp.asarray(np.concatenate([c, c, -s, s], axis=1).astype(np.float32))

    vmem = pl.BlockSpec(memory_space=pltpu.VMEM)
    smem = pl.BlockSpec(memory_space=pltpu.SMEM)
    most = max(olds, slots)
    m = steps * group
    dims = (n, pool, heads, group, plen, cap, rows, packed)
    dma = pltpu.SemaphoreType.DMA
    size = packed // PIECES
    return pl.pallas_call(
        functools.partial(kernel, dims),
        out_shape=(
            jax.ShapeDtypeStruct(query_old.shape, BF16),
            jax.ShapeDtypeStruct(query_new.shape, BF16),
        ),
        in_specs=[vmem, pl.BlockSpec(memory_space=pl.ANY)] + [vmem] * 9 + [smem] * 3,
        out_specs=(vmem, vmem),
        scratch_shapes=[
            pltpu.VMEM((2, kv_weight.shape[0], 2 * HD), BF16),
            pltpu.VMEM((rows, 2 * HD), BF16),
            pltpu.VMEM((PIECES, size, size + rows - packed), BF16),
            pltpu.VMEM((n, heads, packed, 2 * HD), BF16),
            pltpu.VMEM((2, n, heads, packed, 2 * HD), BF16),
            pltpu.VMEM((m * most, HD), F32),
            pltpu.VMEM((16 * most, HD), F32),
            pltpu.VMEM((16 * most, HD), F32),
            pltpu.VMEM((m * most, HD), F32),
            pltpu.VMEM((slots, plen, 2 * HD), BF16),
        ]
        + [pltpu.VMEM((pool, packed, 2 * HD), BF16) for _ in range(heads)]
        + [
            dma((2,)),
            dma((n, heads, PIECES)),
            dma((2, n, heads, PIECES)),
            dma((pool // 2, heads, PIECES)),
            dma((pool, heads, PIECES)),
            dma((pool // 2, heads, PIECES)),
        ],
        compiler_params=pltpu.CompilerParams(
            collective_id=0, has_side_effects=True, vmem_limit_bytes=60 << 20
        ),
    )(
        prompt_states, kv_weight, target, ptab, query_old, step_old, old_cache, tab_old,
        query_new, step_new, tab_new, old_lens[0], off_new, len_new,
    )


def solution(mesh):
    both = ("rep", "pool")
    return jax.shard_map(
        local,
        mesh=mesh,
        in_specs=(
            P(both, "tp"),
            P("tp", None),
            P(both, None),
            P(both, None),
            P(both, None, "tp"),
            P(both, None),
            P(None, both, "tp"),
            P(None, both, "tp"),
            P(None, both, "tp"),
            P(None, both, "tp"),
        ),
        out_specs=(P(None, both, "tp"), P(None, both, "tp")),
        check_vma=False,
    )
```

```python
import functools
import math

import jax
import jax.numpy as jnp
import numpy as np
from jax import lax
from jax.experimental import pallas as pl
from jax.experimental.pallas import tpu as pltpu
from jax.sharding import PartitionSpec as P

HD = 128
PIECES = 3
MESH = pl.DeviceIdType.MESH
F32 = jnp.float32
BF16 = jnp.bfloat16


def turn(v, cosine, sine):
    return v * cosine + pltpu.roll(v, HD // 2, v.ndim - 1) * sine


def tables(pos):
    half = HD // 2
    freq = jnp.exp(-(2.0 * jnp.arange(half, dtype=F32) / HD) * math.log(500000.0))
    angle = pos[..., None].astype(F32) * freq
    c, s = jnp.cos(angle), jnp.sin(angle)
    return jnp.concatenate([c, c, -s, s], axis=-1)


def kernel(
    dims,
    x, w, target, ptab, q_old, s_old, cache, tab_old, q_new, s_new, tab_new,
    len_old, off_new, len_new,
    o_old, o_new,
    wbuf, y, pick, part, rbuf, qs, ks, vs, os_, store, *rest,
):
    n, pool, heads, group, plen, cap, rows, packed = dims
    pbuf = rest[:heads]
    wsem, zsend, zrecv, agsend, agrecv, fwsend = rest[heads:]
    z, me = lax.axis_index("tp"), lax.axis_index("pool")
    chips = pool // 2
    chip, core = me // 2, lax.rem(me, 2)
    mate = chip * 2 + 1 - core
    size = packed // PIECES
    slack = rows - packed
    steps = q_old.shape[0]

    def peer(k):
        return lax.rem(chip + k, chips) * 2 + core

    def source(k):
        return lax.rem(chip + chips - k, chips) * 2 + core

    def order(k):
        middle = n - 1 - k // 2 if k % 2 == 0 else (k - 1) // 2
        return jnp.where(z == 0, n - 1 - k, jnp.where(z == n - 1, k, middle))

    blocks = [(h, k) for h in range(heads) for k in range(n)]

    def weights(i):
        h, k = blocks[i]
        first = pl.multiple_of((order(k) * heads + h) * 2 * HD, 2 * HD)
        return pltpu.make_async_copy(
            w.at[:, pl.ds(first, 2 * HD)], wbuf.at[i % 2], wsem.at[i % 2]
        )

    weights(0).start()

    barrier = pltpu.get_barrier_semaphore()

    @pl.when(z > 0)
    def _():
        pl.semaphore_signal(barrier, inc=1, device_id={"tp": z - 1}, device_id_type=MESH)

    @pl.when(z < n - 1)
    def _():
        pl.semaphore_signal(barrier, inc=1, device_id={"tp": z + 1}, device_id_type=MESH)

    pl.semaphore_signal(barrier, inc=1, device_id={"pool": mate}, device_id_type=MESH)
    for k in range(1, chips):
        pl.semaphore_signal(barrier, inc=1, device_id={"pool": peer(k)}, device_id_type=MESH)
    for p in range(PIECES):
        wanted = target[:, p * size : (p + 1) * size + slack]
        line = lax.broadcasted_iota(jnp.int32, (size, size + slack), 0) + p * size
        pick[p] = jnp.where(line == wanted, 1.0, 0.0).astype(BF16)
    ks[...] = jnp.zeros_like(ks)
    vs[...] = jnp.zeros_like(vs)
    edges = (z > 0).astype(jnp.int32) + (z < n - 1).astype(jnp.int32)
    pl.semaphore_wait(barrier, edges + chips)

    def span(p):
        return pl.ds(p * size, size)

    def up(d, h, p):
        return pltpu.make_async_remote_copy(
            part.at[d, h, span(p)], rbuf.at[0, d, h, span(p)],
            zsend.at[d, h, p], zrecv.at[0, d, h, p],
            device_id={"tp": z + 1}, device_id_type=MESH,
        )

    def down(d, h, p):
        return pltpu.make_async_remote_copy(
            part.at[d, h, span(p)], rbuf.at[1, d, h, span(p)],
            zsend.at[d, h, p], zrecv.at[1, d, h, p],
            device_id={"tp": z - 1}, device_id_type=MESH,
        )

    def share(h, p, k):
        return pltpu.make_async_remote_copy(
            pbuf[h].at[me, span(p)], pbuf[h].at[me, span(p)],
            agsend.at[k, h, p], agrecv.at[me, h, p],
            device_id={"pool": mate if k == 0 else peer(k)}, device_id_type=MESH,
        )

    def forward(h, p, k):
        src = source(k)
        return pltpu.make_async_remote_copy(
            pbuf[h].at[src, span(p)], pbuf[h].at[src, span(p)],
            fwsend.at[k, h, p], agrecv.at[src, h, p],
            device_id={"pool": mate}, device_id_type=MESH,
        )

    def arrived(h, p, src):
        return pltpu.make_async_remote_copy(
            pbuf[h].at[src, span(p)], pbuf[h].at[src, span(p)],
            fwsend.at[0, h, p], agrecv.at[src, h, p],
            device_id={"pool": mate}, device_id_type=MESH,
        )

    def multiply(i):
        h, k = blocks[i]
        d = order(k)
        if i + 1 < len(blocks):
            weights(i + 1).start()
        weights(i).wait()
        tile = 4 * plen

        def body(r, carry):
            at = pl.ds(pl.multiple_of(r * tile, tile), tile)
            got = jnp.dot(x[at, :], wbuf[i % 2], preferred_element_type=F32)
            y[at, HD:] = got[:, HD:].astype(BF16)
            key = got[:, :HD].reshape(4, plen, HD)
            key = turn(key, ptab[:, :HD][None], ptab[:, HD:][None])
            y[at, :HD] = key.reshape(tile, HD).astype(BF16)
            return carry

        lax.fori_loop(0, rows // tile, body, 0)
        for p in range(PIECES):
            part[d, h, span(p)] = jnp.dot(
                pick[p], y[p * size : (p + 1) * size + slack], preferred_element_type=F32
            ).astype(BF16)

            @pl.when((z == 0) & (d > 0))
            def _():
                up(d, h, p).start()

            @pl.when((z == n - 1) & (d < n - 1))
            def _():
                down(d, h, p).start()

    def relay(h, s):
        for p in range(PIECES):
            high, low = n - 1 - s, s

            @pl.when((z > 0) & (z < high))
            def _():
                up(high, h, p).wait_recv()
                part[high, h, span(p)] = (
                    part[high, h, span(p)].astype(F32) + rbuf[0, high, h, span(p)].astype(F32)
                ).astype(BF16)
                up(high, h, p).start()

            @pl.when((z < n - 1) & (z > low))
            def _():
                down(low, h, p).wait_recv()
                part[low, h, span(p)] = (
                    part[low, h, span(p)].astype(F32) + rbuf[1, low, h, span(p)].astype(F32)
                ).astype(BF16)
                down(low, h, p).start()

    def finish(h):
        for p in range(PIECES):
            mine = pbuf[h].at[me, span(p)]

            @pl.when(z == 0)
            def _():
                down(z, h, p).wait_recv()
                mine[...] = (
                    part[z, h, span(p)].astype(F32) + rbuf[1, z, h, span(p)].astype(F32)
                ).astype(BF16)

            @pl.when(z == n - 1)
            def _():
                up(z, h, p).wait_recv()
                mine[...] = (
                    part[z, h, span(p)].astype(F32) + rbuf[0, z, h, span(p)].astype(F32)
                ).astype(BF16)

            @pl.when((z > 0) & (z < n - 1))
            def _():
                up(z, h, p).wait_recv()
                down(z, h, p).wait_recv()
                mine[...] = (
                    part[z, h, span(p)].astype(F32)
                    + rbuf[0, z, h, span(p)].astype(F32)
                    + rbuf[1, z, h, span(p)].astype(F32)
                ).astype(BF16)

            for k in range(chips):
                share(h, p, k).start()

    def spread(h):
        for p in range(PIECES):
            for k in range(1, chips):
                arrived(h, p, source(k)).wait_recv()
                forward(h, p, k).start()

    def collect(h):
        for p in range(PIECES):
            for k in range(chips):
                arrived(h, p, lax.rem(chip + k, chips) * 2 + 1 - core).wait_recv()

    def attend(h, q, st, tab, out, block, width, per, count):
        for t in range(steps):
            c, s = tab[t, :, :HD], tab[t, :, HD:]
            for g in range(group):
                col = (h * group + g) * HD
                at = (t * group + g) * count
                qs[at : at + count, :] = turn(q[t, :, col : col + HD].astype(F32), c, s)
            col = h * 2 * HD
            ks[t * count : (t + 1) * count, :] = turn(st[t, :, col : col + HD].astype(F32), c, s)
            vs[t * count : (t + 1) * count, :] = st[t, :, col + HD : col + 2 * HD].astype(F32)
        if count * steps < ks.shape[0]:
            ks[count * steps :, :] = jnp.zeros((ks.shape[0] - count * steps, HD), F32)
            vs[count * steps :, :] = jnp.zeros((ks.shape[0] - count * steps, HD), F32)
        m = steps * group
        col = lax.broadcasted_iota(jnp.int32, (m, width + 16), 1)
        now = lax.broadcasted_iota(jnp.int32, (m, width + 16), 0) // group
        recent = (col >= width) & (col - width <= now)

        def body(i, carry):
            for j in range(per):
                b = i * per + j
                kv, low, high = block(b, h)
                query = qs[pl.ds(b, m, stride=count), :].astype(BF16)
                own_k = ks[pl.ds(b, 16, stride=count), :].astype(BF16)
                own_v = vs[pl.ds(b, 16, stride=count), :].astype(BF16)
                keys = jnp.concatenate([kv[:, :HD], own_k], axis=0)
                values = jnp.concatenate([kv[:, HD:], own_v], axis=0)
                score = lax.dot_general(
                    query, keys, (((1,), (1,)), ((), ())), preferred_element_type=F32
                ) * (1.0 / math.sqrt(HD))
                keep = ((col >= low) & (col < high)) | recent
                score = jnp.where(keep, score, -1e30)
                top = jnp.max(score, axis=-1, keepdims=True)
                e = jnp.exp(score - top)
                total = jnp.sum(e, axis=-1, keepdims=True)
                got = jnp.dot(e.astype(BF16), values, preferred_element_type=F32) / total
                os_[pl.ds(b, m, stride=count), :] = got
            return carry

        lax.fori_loop(0, count // per, body, 0)
        for t in range(steps):
            for g in range(group):
                c0 = (h * group + g) * HD
                at = (t * group + g) * count
                out[t, :, c0 : c0 + HD] = os_[at : at + count, :].astype(BF16)

    def resident(b, h):
        return cache[b, :, h * 2 * HD : (h + 1) * 2 * HD], 0, len_old[b]

    def placed(b, h):
        return store[b], 0, len_new[b]

    def place(h):
        ahead = lax.broadcasted_iota(jnp.int32, (plen, packed), 1) - lax.broadcasted_iota(
            jnp.int32, (plen, packed), 0
        )

        def body(s, carry):
            got = pbuf[h][s]
            chosen = jnp.concatenate(
                [
                    jnp.where(ahead == off_new[s * cap + j], 1.0, 0.0).astype(BF16)
                    for j in range(cap)
                ],
                axis=0,
            )
            rows_of = jnp.dot(chosen, got, preferred_element_type=F32).astype(BF16)
            for j in range(cap):
                store[s * cap + j] = rows_of[j * plen : (j + 1) * plen]
            return carry

        lax.fori_loop(0, pool, body, 0)

    def old(h):
        attend(h, q_old, s_old, tab_old, o_old, resident, cache.shape[1], 8, q_old.shape[1])

    def new(h):
        collect(h)
        place(h)
        attend(h, q_new, s_new, tab_new, o_new, placed, plen, 8, q_new.shape[1])

    if heads == 2 and n == 4:
        for i in range(3):
            multiply(i)
        relay(0, 0)
        multiply(3)
        multiply(4)
        relay(0, 1)
        multiply(5)
        finish(0)
        multiply(6)
        relay(1, 0)
        multiply(7)
        relay(1, 1)
        spread(0)
        old(0)
        finish(1)
        old(1)
        spread(1)
        new(0)
        new(1)
    else:
        for h in range(heads):
            for k in range(n):
                multiply(h * n + k)
            for at in range(n - 1):
                relay(h, at)
            finish(h)
            spread(h)
            old(h)
        for h in range(heads):
            new(h)

    for h in range(heads):
        for p in range(PIECES):
            for d in range(n):

                @pl.when(z < d)
                def _():
                    up(d, h, p).wait_send()

                @pl.when(z > d)
                def _():
                    down(d, h, p).wait_send()

            for k in range(chips):
                share(h, p, k).wait_send()
            for k in range(1, chips):
                forward(h, p, k).wait_send()


def local(
    prompt_states,
    kv_weight,
    prompt_lens,
    placement,
    old_cache,
    old_lens,
    query_old,
    step_old,
    query_new,
    step_new,
):
    rows = prompt_states.shape[0]
    n, pool = lax.axis_size("tp"), lax.axis_size("pool")
    prompts = prompt_lens.shape[1]
    plen = rows // prompts
    packed = rows * 3 // 4
    heads = kv_weight.shape[1] // n // (2 * HD)
    group = query_old.shape[2] // (heads * HD)
    steps, olds = query_old.shape[:2]
    slots = query_new.shape[1]
    cap = slots // pool

    lens = prompt_lens[0]
    before = jnp.arange(prompts)[:, None] > jnp.arange(prompts)[None]
    begin = jnp.sum(jnp.where(before, lens[None], 0), axis=1)
    k = jnp.arange(plen, dtype=jnp.int32)[None]
    target = jnp.where(k < lens[:, None], begin[:, None] + k, -1).reshape(1, rows)

    meta = lax.all_gather(jnp.stack([lens, placement[:, 0]]), "pool")
    all_lens, dest = meta[:, 0], meta[:, 1]
    all_begin = jnp.sum(jnp.where(before[None], all_lens[:, None], 0), axis=2)
    here = (dest == lax.axis_index("pool")).astype(jnp.int32)
    rank = jnp.sum(jnp.where(before[None], here[:, None], 0), axis=2)
    hit = (here[:, None, :] > 0) & (
        rank[:, None, :] == jnp.arange(cap, dtype=jnp.int32)[None, :, None]
    )
    len_new = jnp.sum(jnp.where(hit, all_lens[:, None], 0), axis=2).reshape(slots)
    off_new = jnp.sum(jnp.where(hit, all_begin[:, None], 0), axis=2).reshape(slots)
    t = jnp.arange(steps, dtype=jnp.int32)[:, None]
    tab_old = tables(old_lens + t)
    tab_new = tables(len_new[None] + t)
    half = HD // 2
    angle = np.arange(plen, dtype=np.float32)[:, None] * np.exp(
        -(2.0 * np.arange(half, dtype=np.float32) / HD) * np.float32(math.log(500000.0))
    ).astype(np.float32)
    c, s = np.cos(angle), np.sin(angle)
    ptab = jnp.asarray(np.concatenate([c, c, -s, s], axis=1).astype(np.float32))

    vmem = pl.BlockSpec(memory_space=pltpu.VMEM)
    smem = pl.BlockSpec(memory_space=pltpu.SMEM)
    most = max(olds, slots)
    m = steps * group
    dims = (n, pool, heads, group, plen, cap, rows, packed)
    dma = pltpu.SemaphoreType.DMA
    size = packed // PIECES
    return pl.pallas_call(
        functools.partial(kernel, dims),
        out_shape=(
            jax.ShapeDtypeStruct(query_old.shape, BF16),
            jax.ShapeDtypeStruct(query_new.shape, BF16),
        ),
        in_specs=[vmem, pl.BlockSpec(memory_space=pl.ANY)] + [vmem] * 9 + [smem] * 3,
        out_specs=(vmem, vmem),
        scratch_shapes=[
            pltpu.VMEM((2, kv_weight.shape[0], 2 * HD), BF16),
            pltpu.VMEM((rows, 2 * HD), BF16),
            pltpu.VMEM((PIECES, size, size + rows - packed), BF16),
            pltpu.VMEM((n, heads, packed, 2 * HD), BF16),
            pltpu.VMEM((2, n, heads, packed, 2 * HD), BF16),
            pltpu.VMEM((m * most, HD), F32),
            pltpu.VMEM((16 * most, HD), F32),
            pltpu.VMEM((16 * most, HD), F32),
            pltpu.VMEM((m * most, HD), F32),
            pltpu.VMEM((slots, plen, 2 * HD), BF16),
        ]
        + [pltpu.VMEM((pool, packed, 2 * HD), BF16) for _ in range(heads)]
        + [
            dma((2,)),
            dma((n, heads, PIECES)),
            dma((2, n, heads, PIECES)),
            dma((pool // 2, heads, PIECES)),
            dma((pool, heads, PIECES)),
            dma((pool // 2, heads, PIECES)),
        ],
        compiler_params=pltpu.CompilerParams(
            collective_id=0, has_side_effects=True, vmem_limit_bytes=60 << 20
        ),
    )(
        prompt_states, kv_weight, target, ptab, query_old, step_old, old_cache, tab_old,
        query_new, step_new, tab_new, old_lens[0], off_new, len_new,
    )


def solution(mesh):
    both = ("rep", "pool")
    return jax.shard_map(
        local,
        mesh=mesh,
        in_specs=(
            P(both, "tp"),
            P("tp", None),
            P(both, None),
            P(both, None),
            P(both, None, "tp"),
            P(both, None),
            P(None, both, "tp"),
            P(None, both, "tp"),
            P(None, both, "tp"),
            P(None, both, "tp"),
        ),
        out_specs=(P(None, both, "tp"), P(None, both, "tp")),
        check_vma=False,
    )
```
